768 devices in a mesh: blk: 192 (over x_lo, y, z), group: 4 (over x_hi, core).
Axes of the slice: x: 4 (x_hi: 2, x_lo: 2; x = x_hi * 2 + x_lo), y: 8, z: 12, core: 2. Of those that a mesh axis runs over, the one named last changes fastest.
Arguments:
- photo_features: float32 [122880, 1152], P(('blk', 'group')), may hold values from -0.1875 to 0.1875
- text_emb: float32 [122880, 1152], P(('blk', 'group')), may hold values from -0.1875 to 0.1875
- sharpness_factor: float32 [1], replicated, may hold values from 30 to 100
- logit_bias: float32 [1], replicated, may hold values from -6 to -2
Outputs:
- photo_feature_derivative: float32 [122880, 1152], P(('blk', 'group'))
- sentence_feature_derivative: float32 [122880, 1152], P(('blk', 'group'))
The draws below stay inside these ranges and needn't reach their ends.
All inputs are finite; a program needn't handle non-finite values.
Results may differ from the reference program's by a relative error of at most 0.0003.
Values sent between devices are 32-bit elements; how exact they have to be, the bound alone decides.
No kernel may reach another device: no remote copies, remote signals or barrier semaphores. Data moves between devices by JAX's collectives and lax.ppermute only.
A program may use at most 64 MiB of HBM per device.

```python
import math
import jax
import jax.numpy as jnp
from jax import lax

FEATURE_DEPTH = 1152
BLK_ROWS = 640
MATCH_COUNT = 122880
N_BLK = 192


def level_of(own_key, shape, split, smallest, top_value):
    loudness, own = 1.0, jax.random.fold_in(own_key, 6)
    for dim, blocks in split:
        steps = jnp.exp(jax.random.uniform(jax.random.fold_in(own, dim), (blocks,), jnp.float32, smallest / len(split), top_value / len(split)))
        loudness = loudness * jnp.repeat(steps, shape[dim] // blocks).reshape([-1 if axis == dim else 1 for axis in range(len(shape))])
    return loudness


def noise(own_key, extent, spread, reach, pieces=(), kind=jnp.bfloat16):
    level = level_of(own_key, extent, pieces, -0.22, 0.18) if pieces else 1.0
    result = jax.random.normal(own_key, extent, jnp.float32) * spread * level
    return jnp.minimum(jnp.maximum(result, -reach), reach).astype(kind)


def setup_inputs(seed: int = 0) -> dict:
    arg_keys = jax.random.split(jax.random.key(seed), 5)
    photo_features = noise(arg_keys[0], (MATCH_COUNT, FEATURE_DEPTH), 0.03, 0.1875, ((0, 768),), jnp.float32)
    text_emb = noise(arg_keys[1], (MATCH_COUNT, FEATURE_DEPTH), 0.03, 0.1875, ((0, 768),), jnp.float32)
    sharpness_factor = jnp.clip(jnp.exp(jax.random.uniform(arg_keys[2], (1,), jnp.float32, math.log(30.0), math.log(100.0))), 30.0, 100.0)
    logit_bias = jnp.clip(jax.random.uniform(arg_keys[3], (1,), jnp.float32, -6.0, -2.0), -6.0, -2.0)
    return {"photo_features": photo_features, "text_emb": text_emb, "sharpness_factor": sharpness_factor, "logit_bias": logit_bias}


def cross_similarity_derivatives(left_operand_features, right_operand_features, scaled_sharpness, segment_offset):
    similarity_matrix = scaled_sharpness * jnp.dot(left_operand_features, right_operand_features.T, precision=lax.Precision.HIGHEST, preferred_element_type=jnp.float32) + segment_offset
    row_ids = jnp.arange(left_operand_features.shape[0], dtype=jnp.int32)[:, None]
    col_ids = jnp.arange(right_operand_features.shape[0], dtype=jnp.int32)[None, :]
    match_polarity = jnp.where(row_ids + BLK_ROWS == col_ids, jnp.float32(1.0), jnp.float32(-1.0))
    return -match_polarity * jax.nn.sigmoid(-match_polarity * similarity_matrix) * scaled_sharpness


def neighbourhood_derivative(resident_segments, remote_segments, scaled_sharpness, segment_offset):
    def one_position(position):
        lower = jnp.mod(position - 1 + N_BLK, N_BLK).astype(jnp.int32)
        upper = jnp.mod(position + 1, N_BLK).astype(jnp.int32)
        left_operand_features = lax.dynamic_index_in_dim(resident_segments, position, 0, keepdims=False)
        right_operand_features = jnp.concatenate([
            lax.dynamic_index_in_dim(remote_segments, lower, 0, keepdims=False),
            lax.dynamic_index_in_dim(remote_segments, position, 0, keepdims=False),
            lax.dynamic_index_in_dim(remote_segments, upper, 0, keepdims=False)], axis=0)
        objective_derivatives = cross_similarity_derivatives(left_operand_features, right_operand_features, scaled_sharpness, segment_offset)
        return jnp.dot(objective_derivatives, right_operand_features, precision=lax.Precision.HIGHEST, preferred_element_type=jnp.float32)
    return lax.map(one_position, jnp.arange(N_BLK, dtype=jnp.int32))


def reference(photo_features, text_emb, sharpness_factor, logit_bias):
    photo_segment_group = photo_features.reshape(N_BLK, BLK_ROWS, FEATURE_DEPTH)
    sentence_segment_group = text_emb.reshape(N_BLK, BLK_ROWS, FEATURE_DEPTH)
    scaled_sharpness = sharpness_factor[0]
    segment_offset = logit_bias[0]
    photo_feature_derivative = neighbourhood_derivative(photo_segment_group, sentence_segment_group, scaled_sharpness, segment_offset).reshape(MATCH_COUNT, FEATURE_DEPTH)
    sentence_feature_derivative = neighbourhood_derivative(sentence_segment_group, photo_segment_group, scaled_sharpness, segment_offset).reshape(MATCH_COUNT, FEATURE_DEPTH)
    return photo_feature_derivative, sentence_feature_derivative
```

```python
import jax
import jax.numpy as jnp
from jax import lax
from jax.sharding import PartitionSpec as P

AXES = ("blk", "group")


def routes(mesh):
    positions, members = mesh.shape["blk"], mesh.shape["group"]
    forward, across, sibling = [], [], []
    for b in range(positions):
        for g in range(members):
            half, core = divmod(g, 2)
            turn = (b + 1) % (positions // 2) == 0
            landing = (1 - half if turn and core == 1 else half) * 2 + core
            here = b * members + g
            forward.append((here, (b + 1) % positions * members + landing))
            across.append((here, b * members + (1 - half) * 2 + core))
            sibling.append((here, b * members + half * 2 + 1 - core))
    backward = [(target, source) for source, target in forward]
    return forward, backward, across, sibling


def dot(a, b, dims):
    return lax.dot_general(a, b, (dims, ((), ())), precision=lax.Precision.HIGH, preferred_element_type=jnp.float32)


def solution(mesh):
    forward, backward, across, sibling = routes(mesh)

    def move(x, pairs):
        return lax.ppermute(x, AXES, pairs)

    def shards(photo, text, sharpness, bias):
        rows = photo.shape[0]
        scale, offset = sharpness[0], bias[0]
        below = move(text, forward)
        above = move(text, backward)
        far = move(photo, across)
        near = move(photo, sibling)
        far_near = move(far, sibling)
        texts = jnp.concatenate([below, text, above], axis=0)
        r = jnp.arange(2 * rows, dtype=jnp.int32)[:, None]
        c = jnp.arange(3 * rows, dtype=jnp.int32)[None, :]
        match = r + rows == c

        def slopes(left, diagonal):
            logit = scale * dot(left, texts, ((1,), (1,))) + offset
            if diagonal:
                label = jnp.where(match & (r < rows), jnp.float32(1), jnp.float32(-1))
                return -label * jax.nn.sigmoid(-label * logit) * scale
            return jax.nn.sigmoid(logit) * scale

        far2 = jnp.concatenate([far, far_near], axis=0)
        near2 = jnp.concatenate([photo, near], axis=0)
        g_far = slopes(far2, False)
        p_far = dot(g_far, texts, ((1,), (0,)))
        far_near_back = move(p_far[rows:], sibling)
        far_back = move(p_far[:rows] + far_near_back, across)
        g_near = slopes(near2, True)
        g = jnp.concatenate([g_near, g_far], axis=0)
        p = jnp.concatenate([near2, far2], axis=0)
        t = dot(g, p, ((0,), (0,)))
        t_below = move(t[:rows], backward)
        t_above = move(t[2 * rows :], forward)
        p_near = dot(g_near, texts, ((1,), (0,)))
        near_back = move(p_near[rows:], sibling)
        return p_near[:rows] + near_back + far_back, t[rows : 2 * rows] + t_below + t_above

    spec = P(AXES, None)
    return jax.shard_map(shards, mesh=mesh, in_specs=(spec, spec, P(), P()), out_specs=(spec, spec), check_vma=False)
```

```python
import jax
import jax.numpy as jnp
from jax import lax
from jax.sharding import PartitionSpec as P

AXES = ("blk", "group")


def routes(mesh):
    positions, members = mesh.shape["blk"], mesh.shape["group"]
    forward, across, sibling = [], [], []
    for b in range(positions):
        for g in range(members):
            half, core = divmod(g, 2)
            turn = (b + 1) % (positions // 2) == 0
            landing = (1 - half if turn and core == 1 else half) * 2 + core
            here = b * members + g
            forward.append((here, (b + 1) % positions * members + landing))
            across.append((here, b * members + (1 - half) * 2 + core))
            sibling.append((here, b * members + half * 2 + 1 - core))
    backward = [(target, source) for source, target in forward]
    return forward, backward, across, sibling


def dot(a, b, dims):
    return lax.dot_general(a, b, (dims, ((), ())), precision=lax.Precision.HIGH, preferred_element_type=jnp.float32)


def after(value, *earlier):
    return lax.optimization_barrier((value, *earlier))[0]


def solution(mesh):
    forward, backward, across, sibling = routes(mesh)

    def move(x, pairs):
        return lax.ppermute(x, AXES, pairs)

    def shards(photo, text, sharpness, bias):
        rows = photo.shape[0]
        scale, offset = sharpness[0], bias[0]
        text_f = move(text, forward)
        text_b = move(text, backward)
        far = move(photo, across)
        near = move(photo, sibling)
        far_near = move(far, sibling)
        p = jnp.concatenate([photo, near, far, far_near], axis=0)
        texts = jnp.concatenate([text, text_f, text_b], axis=0)
        r = jnp.arange(4 * rows, dtype=jnp.int32)[:, None]
        c = jnp.arange(3 * rows, dtype=jnp.int32)[None, :]
        label = jnp.where((r == c) & (r < rows), jnp.float32(1), jnp.float32(-1))
        logit = scale * dot(p, texts, ((1,), (1,))) + offset
        g = -label * jax.nn.sigmoid(-label * logit) * scale
        p_far = dot(g[2 * rows :], texts, ((1,), (0,)))
        far_near_back = move(p_far[rows:], sibling)
        t_b = dot(after(g, p_far)[:, 2 * rows :], p, ((0,), (0,)))
        b_back = move(t_b, forward)
        p_across = p_far[:rows] + after(far_near_back, t_b)
        far_back = move(p_across, across)
        g = after(g, p_across)
        p_near = dot(g[: 2 * rows], texts, ((1,), (0,)))
        near_back = move(p_near[rows:], sibling)
        t_f = dot(after(g, p_near)[:, rows : 2 * rows], p, ((0,), (0,)))
        f_back = move(t_f, backward)
        t_own = dot(after(g, t_f)[:, :rows], p, ((0,), (0,))) + b_back
        p_own = p_near[:rows] + near_back + after(far_back, t_own)
        return p_own, t_own + after(f_back, p_own)

    spec = P(AXES, None)
    return jax.shard_map(shards, mesh=mesh, in_specs=(spec, spec, P(), P()), out_specs=(spec, spec), check_vma=False)
```

```python
import jax
import jax.numpy as jnp
from jax import lax
from jax.sharding import PartitionSpec as P

AXES = ("blk", "group")


def routes(mesh):
    positions, members = mesh.shape["blk"], mesh.shape["group"]
    forward, across, sibling = [], [], []
    for b in range(positions):
        for g in range(members):
            half, core = divmod(g, 2)
            turn = (b + 1) % (positions // 2) == 0
            landing = (1 - half if turn and core == 1 else half) * 2 + core
            here = b * members + g
            forward.append((here, (b + 1) % positions * members + landing))
            across.append((here, b * members + (1 - half) * 2 + core))
            sibling.append((here, b * members + half * 2 + 1 - core))
    backward = [(target, source) for source, target in forward]
    return forward, backward, across, sibling


def dot(a, b, dims):
    return lax.dot_general(a, b, (dims, ((), ())), precision=lax.Precision.HIGH, preferred_element_type=jnp.float32)


def after(value, *earlier):
    return lax.optimization_barrier((value, *earlier))[0]


def solution(mesh):
    forward, backward, across, sibling = routes(mesh)

    def move(x, pairs):
        return lax.ppermute(x, AXES, pairs)

    def shards(photo, text, sharpness, bias):
        rows = photo.shape[0]
        scale, offset = sharpness[0], bias[0]
        text_f = move(text, forward)
        text_b = move(text, backward)
        far = move(photo, across)
        near = move(photo, sibling)
        pass
        far_near = move(far, sibling)
        p = jnp.concatenate([photo, far, far_near, near], axis=0)
        texts = jnp.concatenate([text, text_f, text_b], axis=0)
        r = jnp.arange(4 * rows, dtype=jnp.int32)[:, None]
        c = jnp.arange(3 * rows, dtype=jnp.int32)[None, :]
        label = jnp.where((r == c) & (r < rows), jnp.float32(1), jnp.float32(-1))
        logit = scale * dot(p, texts, ((1,), (1,))) + offset
        g = -label * jax.nn.sigmoid(-label * logit) * scale
        p_far = dot(g[rows : 3 * rows], texts, ((1,), (0,)))
        far_near_back = move(p_far[rows:], sibling)
        t_fb = dot(after(g, p_far)[:, rows:], p, ((0,), (0,)))
        b_back = move(t_fb[rows:], forward)
        p_across = p_far[:rows] + after(far_near_back, t_fb)
        far_back = move(p_across, across)
        f_back = move(after(t_fb[:rows], p_across), backward)
        g = after(g, p_across)
        p_near = dot(g[3 * rows :], texts, ((1,), (0,)))
        near_back = move(p_near, sibling)
        g = after(g, p_near)
        p_own = dot(g[:rows], texts, ((1,), (0,)))
        t_own = dot(after(g, p_own)[:, :rows], p, ((0,), (0,)))
        t_sum = t_own + b_back + f_back
        return p_own + near_back + after(far_back, t_sum), t_sum

    spec = P(AXES, None)
    return jax.shard_map(shards, mesh=mesh, in_specs=(spec, spec, P(), P()), out_specs=(spec, spec), check_vma=False)
```

```python
import jax
import jax.numpy as jnp
from jax import lax
from jax.sharding import PartitionSpec as P

AXES = ("blk", "group")


def routes(mesh):
    positions, members = mesh.shape["blk"], mesh.shape["group"]
    forward, across, sibling = [], [], []
    for b in range(positions):
        for g in range(members):
            half, core = divmod(g, 2)
            turn = (b + 1) % (positions // 2) == 0
            landing = (1 - half if turn and core == 1 else half) * 2 + core
            here = b * members + g
            forward.append((here, (b + 1) % positions * members + landing))
            across.append((here, b * members + (1 - half) * 2 + core))
            sibling.append((here, b * members + half * 2 + 1 - core))
    backward = [(target, source) for source, target in forward]
    return forward, backward, across, sibling


def dot(a, b, dims):
    return lax.dot_general(a, b, (dims, ((), ())), precision=lax.Precision.HIGH, preferred_element_type=jnp.float32)


def after(value, *earlier):
    return lax.optimization_barrier((value, *earlier))[0]


def solution(mesh):
    forward, backward, across, sibling = routes(mesh)

    def move(x, pairs):
        return lax.ppermute(x, AXES, pairs)

    def shards(photo, text, sharpness, bias):
        rows = photo.shape[0]
        scale, offset = sharpness[0], bias[0]
        text_f = move(text, forward)
        text_b = move(text, backward)
        far = move(photo, across)
        near = move(photo, sibling)
        far_near = move(far, sibling)
        texts = jnp.concatenate([text, text_f, text_b], axis=0)
        p = jnp.concatenate([photo, far, far_near, near], axis=0)
        r = jnp.arange(4 * rows, dtype=jnp.int32)[:, None]
        c = jnp.arange(3 * rows, dtype=jnp.int32)[None, :]
        label = jnp.where((r == c) & (r < rows), jnp.float32(1), jnp.float32(-1))
        logit = scale * dot(p, texts, ((1,), (1,))) + offset
        g = -label * jax.nn.sigmoid(-label * logit) * scale
        p_far = dot(g[rows : 3 * rows], texts, ((1,), (0,)))
        far_near_back = move(p_far[rows:], sibling)
        t_fb = dot(after(g, p_far)[:, rows:], p, ((0,), (0,)))
        b_back = move(t_fb[rows:], forward)
        p_across = p_far[:rows] + after(far_near_back, t_fb)
        far_back = move(p_across, across)
        f_back = move(after(t_fb[:rows], p_across), backward)
        t_own = dot(g[:, :rows], p, ((0,), (0,))) + b_back
        g = after(g, t_own)
        p_near = dot(g[3 * rows :], texts, ((1,), (0,)))
        near_back = move(p_near, sibling)
        p_own = dot(g[:rows], texts, ((1,), (0,))) + far_back
        f_back, p_own = lax.optimization_barrier((f_back, p_own))
        t_sum = t_own + f_back
        return p_own + after(near_back, t_sum), t_sum

    spec = P(AXES, None)
    return jax.shard_map(shards, mesh=mesh, in_specs=(spec, spec, P(), P()), out_specs=(spec, spec), check_vma=False)
```

```python
import jax
import jax.numpy as jnp
from jax import lax
from jax.sharding import PartitionSpec as P

AXES = ("blk", "group")


def routes(mesh):
    positions, members = mesh.shape["blk"], mesh.shape["group"]
    forward, across, sibling = [], [], []
    for b in range(positions):
        for g in range(members):
            half, core = divmod(g, 2)
            turn = (b + 1) % (positions // 2) == 0
            landing = (1 - half if turn and core == 1 else half) * 2 + core
            here = b * members + g
            forward.append((here, (b + 1) % positions * members + landing))
            across.append((here, b * members + (1 - half) * 2 + core))
            sibling.append((here, b * members + half * 2 + 1 - core))
    backward = [(target, source) for source, target in forward]
    return forward, backward, across, sibling


def dot(a, b, dims):
    return lax.dot_general(a, b, (dims, ((), ())), precision=lax.Precision.HIGH, preferred_element_type=jnp.float32)


def after(value, *earlier):
    return lax.optimization_barrier((value, *earlier))[0]


def solution(mesh):
    forward, backward, across, sibling = routes(mesh)

    def move(x, pairs):
        return lax.ppermute(x, AXES, pairs)

    def shards(photo, text, sharpness, bias):
        rows = photo.shape[0]
        scale, offset = sharpness[0], bias[0]
        text_f = move(text, forward)
        text_b = move(text, backward)
        far = move(photo, across)
        near = move(photo, sibling)
        far_near = move(far, sibling)
        texts = jnp.concatenate([text, text_f, text_b], axis=0)
        p = jnp.concatenate([photo, far, far_near, near], axis=0)
        r = jnp.arange(4 * rows, dtype=jnp.int32)[:, None]
        c = jnp.arange(3 * rows, dtype=jnp.int32)[None, :]
        label = jnp.where((r == c) & (r < rows), jnp.float32(1), jnp.float32(-1))
        logit = scale * dot(p, texts, ((1,), (1,))) + offset
        g = -label * jax.nn.sigmoid(-label * logit) * scale
        p_far = dot(g[rows : 3 * rows], texts, ((1,), (0,)))
        far_near_back = move(p_far[rows:], sibling)
        t_fb = dot(after(g, p_far)[:, rows:], p, ((0,), (0,)))
        b_back = move(t_fb[rows:], forward)
        p_across = p_far[:rows] + after(far_near_back, t_fb)
        far_back = move(p_across, across)
        f_back = move(after(t_fb[:rows], p_across), backward)
        g = after(g, p_across)
        p_near = dot(g[3 * rows :], texts, ((1,), (0,)))
        near_back = move(p_near, sibling)
        g = after(g, p_near)
        p_own = dot(g[:rows], texts, ((1,), (0,)))
        t_own = dot(after(g, p_own)[:, :rows], p, ((0,), (0,)))
        t_own, b_back, far_back, f_back = lax.optimization_barrier((t_own, b_back, far_back, f_back))
        return p_own + near_back + far_back, t_own + b_back + f_back

    spec = P(AXES, None)
    return jax.shard_map(shards, mesh=mesh, in_specs=(spec, spec, P(), P()), out_specs=(spec, spec), check_vma=False)
```

```python
import jax
import jax.numpy as jnp
from jax import lax
from jax.sharding import PartitionSpec as P

AXES = ("blk", "group")
RING = 12


def routes(mesh):
    positions, members = mesh.shape["blk"], mesh.shape["group"]
    forward, across, sibling = [], [], []
    for b in range(positions):
        for g in range(members):
            half, core = divmod(g, 2)
            turn = (b + 1) % (positions // 2) == 0
            landing = (1 - half if turn and core == 1 else half) * 2 + core
            here = b * members + g
            forward.append((here, (b + 1) % positions * members + landing))
            across.append((here, b * members + (1 - half) * 2 + core))
            sibling.append((here, b * members + half * 2 + 1 - core))
    backward = [(target, source) for source, target in forward]
    return forward, backward, across, sibling


def dot(a, b, dims):
    return lax.dot_general(a, b, (dims, ((), ())), precision=lax.Precision.HIGH, preferred_element_type=jnp.float32)


def after(value, *earlier):
    return lax.optimization_barrier((value, *earlier))[0]


def solution(mesh):
    forward, backward, across, sibling = routes(mesh)
    members = mesh.shape["group"]

    def parted(pairs, first):
        return [pair for pair in pairs if first(*pair)], [pair for pair in pairs if not first(*pair)]

    def wraps(source, target):
        return {source // members % RING, target // members % RING} == {0, RING - 1}

    forward_wrap, forward_in = parted(forward, wraps)
    backward_wrap, backward_in = parted(backward, wraps)
    across_first, across_rest = parted(across, lambda source, target: source // members % RING == 0)

    def move(x, pairs):
        return lax.ppermute(x, AXES, pairs)

    def shards(photo, text, sharpness, bias):
        rows = photo.shape[0]
        scale, offset = sharpness[0], bias[0]
        text_f = move(text, forward)
        text_b = move(text, backward)
        far = move(photo, across)
        near = move(photo, sibling)
        far_near = move(far, sibling)
        texts = jnp.concatenate([text, text_f, text_b], axis=0)
        p = jnp.concatenate([photo, far, far_near, near], axis=0)
        r = jnp.arange(4 * rows, dtype=jnp.int32)[:, None]
        c = jnp.arange(3 * rows, dtype=jnp.int32)[None, :]
        label = jnp.where((r == c) & (r < rows), jnp.float32(1), jnp.float32(-1))
        logit = scale * dot(p, texts, ((1,), (1,))) + offset
        g = -label * jax.nn.sigmoid(-label * logit) * scale
        p_far = dot(g[rows : 3 * rows], texts, ((1,), (0,)))
        far_near_back = move(p_far[rows:], sibling)
        t_fb = dot(after(g, p_far)[:, rows:], p, ((0,), (0,)))
        p_across = p_far[:rows] + after(far_near_back, t_fb)
        far_back = move(p_across, across_first)
        b_back = move(after(t_fb[rows:], p_across), forward)
        f_back = move(after(t_fb[:rows], p_across), backward)
        g = after(g, p_across)
        p_near = dot(g[3 * rows :], texts, ((1,), (0,)))
        far_back_rest = move(after(p_across, p_near), across_rest)
        near_back = move(p_near, sibling)
        g = after(g, p_near)
        p_own = dot(g[:rows], texts, ((1,), (0,)))
        t_own = dot(after(g, p_own)[:, :rows], p, ((0,), (0,)))
        t_sum = after(t_own, p_own) + after(b_back, far_back)
        t_sum = t_sum + after(f_back, t_sum)
        far_back_rest = after(far_back_rest, t_sum)
        return p_own + near_back + far_back + far_back_rest, t_sum

    spec = P(AXES, None)
    return jax.shard_map(shards, mesh=mesh, in_specs=(spec, spec, P(), P()), out_specs=(spec, spec), check_vma=False)
```

```python
import jax
import jax.numpy as jnp
from jax import lax
from jax.sharding import PartitionSpec as P

AXES = ("blk", "group")
RING = 12


def routes(mesh):
    positions, members = mesh.shape["blk"], mesh.shape["group"]
    forward, across, sibling = [], [], []
    for b in range(positions):
        for g in range(members):
            half, core = divmod(g, 2)
            turn = (b + 1) % (positions // 2) == 0
            landing = (1 - half if turn and core == 1 else half) * 2 + core
            here = b * members + g
            forward.append((here, (b + 1) % positions * members + landing))
            across.append((here, b * members + (1 - half) * 2 + core))
            sibling.append((here, b * members + half * 2 + 1 - core))
    backward = [(target, source) for source, target in forward]
    return forward, backward, across, sibling


def dot(a, b, dims):
    return lax.dot_general(a, b, (dims, ((), ())), precision=lax.Precision.HIGH, preferred_element_type=jnp.float32)


def after(value, *earlier):
    return lax.optimization_barrier((value, *earlier))[0]


def solution(mesh):
    forward, backward, across, sibling = routes(mesh)
    members = mesh.shape["group"]

    def parted(pairs, first):
        return [pair for pair in pairs if first(*pair)], [pair for pair in pairs if not first(*pair)]

    def wraps(source, target):
        return {source // members % RING, target // members % RING} == {0, RING - 1}

    forward_wrap, forward_in = parted(forward, wraps)
    backward_wrap, backward_in = parted(backward, wraps)
    across_first, across_rest = parted(across, lambda source, target: source // members % RING == 0)

    def move(x, pairs):
        return lax.ppermute(x, AXES, pairs)

    def shards(photo, text, sharpness, bias):
        rows = photo.shape[0]
        scale, offset = sharpness[0], bias[0]
        text_f = move(text, forward)
        text_b = move(text, backward)
        far = move(photo, across)
        near = move(photo, sibling)
        far_near = move(far, sibling)
        p = jnp.concatenate([photo, far, far_near, near], axis=0)
        r = jnp.arange(4 * rows, dtype=jnp.int32)[:, None]
        c = jnp.arange(2 * rows, dtype=jnp.int32)[None, :]
        label = jnp.where((r == c) & (r < rows), jnp.float32(1), jnp.float32(-1))
        texts = jnp.concatenate([text, text_f], axis=0)
        logit = scale * dot(p, texts, ((1,), (1,))) + offset
        g = -label * jax.nn.sigmoid(-label * logit) * scale
        text_b, g = lax.optimization_barrier((text_b, g))
        logit = scale * dot(p, text_b, ((1,), (1,))) + offset
        g = jnp.concatenate([g, jax.nn.sigmoid(logit) * scale], axis=1)
        texts = jnp.concatenate([texts, text_b], axis=0)
        p_far = dot(g[rows : 3 * rows], texts, ((1,), (0,)))
        far_near_back = move(p_far[rows:], sibling)
        t_fb = dot(g[:, rows:], p, ((0,), (0,)))
        b_back = move(t_fb[rows:], forward)
        p_across = p_far[:rows] + after(far_near_back, t_fb)
        far_back = move(p_across, across_first)
        f_back = move(after(t_fb[:rows], p_across), backward)
        g = after(g, p_across)
        p_near = dot(g[3 * rows :], texts, ((1,), (0,)))
        far_back_rest = move(after(p_across, p_near), across_rest)
        near_back = move(p_near, sibling)
        g = after(g, p_near)
        p_own = dot(g[:rows], texts, ((1,), (0,)))
        t_own = dot(after(g, p_own)[:, :rows], p, ((0,), (0,)))
        t_sum = after(t_own, p_own) + after(b_back, far_back)
        t_sum = t_sum + after(f_back, t_sum)
        far_back_rest = after(far_back_rest, t_sum)
        return p_own + near_back + far_back + far_back_rest, t_sum

    spec = P(AXES, None)
    return jax.shard_map(shards, mesh=mesh, in_specs=(spec, spec, P(), P()), out_specs=(spec, spec), check_vma=False)
```

```python
import jax
import jax.numpy as jnp
from jax import lax
from jax.sharding import PartitionSpec as P

AXES = ("blk", "group")
RING = 12


def routes(mesh):
    positions, members = mesh.shape["blk"], mesh.shape["group"]
    forward, across, sibling = [], [], []
    for b in range(positions):
        for g in range(members):
            half, core = divmod(g, 2)
            turn = (b + 1) % (positions // 2) == 0
            landing = (1 - half if turn and core == 1 else half) * 2 + core
            here = b * members + g
            forward.append((here, (b + 1) % positions * members + landing))
            across.append((here, b * members + (1 - half) * 2 + core))
            sibling.append((here, b * members + half * 2 + 1 - core))
    backward = [(target, source) for source, target in forward]
    return forward, backward, across, sibling


def dot(a, b, dims):
    return lax.dot_general(a, b, (dims, ((), ())), precision=lax.Precision.HIGH, preferred_element_type=jnp.float32)


def after(value, *earlier):
    return lax.optimization_barrier((value, *earlier))[0]


def solution(mesh):
    forward, backward, across, sibling = routes(mesh)
    members = mesh.shape["group"]

    def parted(pairs, first):
        return [pair for pair in pairs if first(*pair)], [pair for pair in pairs if not first(*pair)]

    def wraps(source, target):
        return {source // members % RING, target // members % RING} == {0, RING - 1}

    forward_wrap, forward_in = parted(forward, wraps)
    backward_wrap, backward_in = parted(backward, wraps)
    across_first, across_rest = parted(across, lambda source, target: source // members % RING == 0)

    def move(x, pairs):
        return lax.ppermute(x, AXES, pairs)

    def shards(photo, text, sharpness, bias):
        rows = photo.shape[0]
        scale, offset = sharpness[0], bias[0]
        text_f = move(text, forward)
        text_b = move(text, backward)
        far = move(photo, across)
        near = move(photo, sibling)
        far_near = move(far, sibling)
        p = jnp.concatenate([photo, far, far_near, near], axis=0)
        r = jnp.arange(4 * rows, dtype=jnp.int32)[:, None]
        c = jnp.arange(2 * rows, dtype=jnp.int32)[None, :]
        label = jnp.where((r == c) & (r < rows), jnp.float32(1), jnp.float32(-1))
        texts = jnp.concatenate([text, text_f], axis=0)
        logit = scale * dot(p, texts, ((1,), (1,))) + offset
        g = -label * jax.nn.sigmoid(-label * logit) * scale
        text_b, g = lax.optimization_barrier((text_b, g))
        logit = scale * dot(p, text_b, ((1,), (1,))) + offset
        g = jnp.concatenate([g, jax.nn.sigmoid(logit) * scale], axis=1)
        texts = jnp.concatenate([texts, text_b], axis=0)
        p_far = dot(g[rows : 3 * rows], texts, ((1,), (0,)))
        far_near_back = move(p_far[rows:], sibling)
        t_fb = dot(g[:, rows:], p, ((0,), (0,)))
        p_across = p_far[:rows] + after(far_near_back, t_fb)
        far_back = move(p_across, across_first)
        b_back = move(after(t_fb[rows:], p_across), forward)
        f_back = move(after(t_fb[:rows], p_across), backward)
        g = after(g, p_across)
        p_near = dot(g[3 * rows :], texts, ((1,), (0,)))
        far_back_rest = move(after(p_across, p_near), across_rest)
        near_back = move(p_near, sibling)
        g = after(g, p_near)
        p_own = dot(g[:rows], texts, ((1,), (0,)))
        t_own = dot(after(g, p_own)[:, :rows], p, ((0,), (0,)))
        t_sum = after(t_own, p_own) + after(b_back, far_back)
        t_sum = t_sum + after(f_back, t_sum)
        far_back_rest = after(far_back_rest, t_sum)
        return p_own + near_back + far_back + far_back_rest, t_sum

    spec = P(AXES, None)
    return jax.shard_map(shards, mesh=mesh, in_specs=(spec, spec, P(), P()), out_specs=(spec, spec), check_vma=False)
```

```python
import jax
import jax.numpy as jnp
from jax import lax
from jax.sharding import PartitionSpec as P

AXES = ("blk", "group")
RING = 12


def routes(mesh):
    positions, members = mesh.shape["blk"], mesh.shape["group"]
    forward, across, sibling = [], [], []
    for b in range(positions):
        for g in range(members):
            half, core = divmod(g, 2)
            turn = (b + 1) % (positions // 2) == 0
            landing = (1 - half if turn and core == 1 else half) * 2 + core
            here = b * members + g
            forward.append((here, (b + 1) % positions * members + landing))
            across.append((here, b * members + (1 - half) * 2 + core))
            sibling.append((here, b * members + half * 2 + 1 - core))
    backward = [(target, source) for source, target in forward]
    return forward, backward, across, sibling


def dot(a, b, dims):
    return lax.dot_general(a, b, (dims, ((), ())), precision=lax.Precision.HIGH, preferred_element_type=jnp.float32)


def after(value, *earlier):
    return lax.optimization_barrier((value, *earlier))[0]


def solution(mesh):
    forward, backward, across, sibling = routes(mesh)
    members = mesh.shape["group"]

    def parted(pairs, first):
        return [pair for pair in pairs if first(*pair)], [pair for pair in pairs if not first(*pair)]

    def wraps(source, target):
        return {source // members % RING, target // members % RING} == {0, RING - 1}

    forward_wrap, forward_in = parted(forward, wraps)
    backward_wrap, backward_in = parted(backward, wraps)
    across_first, across_rest = parted(across, lambda source, target: source // members % RING == 0)

    def move(x, pairs):
        return lax.ppermute(x, AXES, pairs)

    def shards(photo, text, sharpness, bias):
        rows = photo.shape[0]
        scale, offset = sharpness[0], bias[0]
        text_f = move(text, forward)
        text_b = move(text, backward)
        far = move(photo, across)
        near = move(photo, sibling)
        far_near = move(far, sibling)
        texts = jnp.concatenate([text, text_f, text_b], axis=0)
        p = jnp.concatenate([photo, far, far_near, near], axis=0)
        r = jnp.arange(4 * rows, dtype=jnp.int32)[:, None]
        c = jnp.arange(3 * rows, dtype=jnp.int32)[None, :]
        label = jnp.where((r == c) & (r < rows), jnp.float32(1), jnp.float32(-1))
        logit = scale * dot(p, texts, ((1,), (1,))) + offset
        g = -label * jax.nn.sigmoid(-label * logit) * scale
        p_far = dot(g[rows : 3 * rows], texts, ((1,), (0,)))
        far_near_back = move(p_far[rows:], sibling)
        t_fb = dot(after(g, p_far)[:, rows:], p, ((0,), (0,)))
        p_across = p_far[:rows] + after(far_near_back, t_fb)
        far_back = move(p_across, across_first)
        b_back = move(after(t_fb[rows:], p_across), forward)
        f_back = move(after(t_fb[:rows], p_across), backward)
        g = after(g, p_across)
        p_near = dot(g[3 * rows :], texts, ((1,), (0,)))
        far_back_rest = move(after(p_across, p_near), across_rest)
        near_back = move(p_near, sibling)
        g = after(g, p_near)
        p_own = dot(g[:rows], texts, ((1,), (0,)))
        t_own = dot(after(g, p_own)[:, :rows], p, ((0,), (0,)))
        t_own, p_own = lax.optimization_barrier((t_own, p_own))
        t_sum = t_own + b_back
        t_sum = t_sum + after(f_back, t_sum)
        far_back = after(far_back, t_sum)
        far_back_rest = after(far_back_rest, far_back)
        return p_own + near_back + far_back + far_back_rest, t_sum

    spec = P(AXES, None)
    return jax.shard_map(shards, mesh=mesh, in_specs=(spec, spec, P(), P()), out_specs=(spec, spec), check_vma=False)
```

```python
import jax
import jax.numpy as jnp
from jax import lax
from jax.sharding import PartitionSpec as P

AXES = ("blk", "group")


def routes(mesh):
    positions, members = mesh.shape["blk"], mesh.shape["group"]
    forward, across, sibling = [], [], []
    for b in range(positions):
        for g in range(members):
            half, core = divmod(g, 2)
            turn = (b + 1) % (positions // 2) == 0
            landing = (1 - half if turn and core == 1 else half) * 2 + core
            here = b * members + g
            forward.append((here, (b + 1) % positions * members + landing))
            across.append((here, b * members + (1 - half) * 2 + core))
            sibling.append((here, b * members + half * 2 + 1 - core))
    backward = [(target, source) for source, target in forward]
    return forward, backward, across, sibling


def dot(a, b, dims):
    return lax.dot_general(a, b, (dims, ((), ())), precision=lax.Precision.HIGH, preferred_element_type=jnp.float32)


def after(value, *earlier):
    return lax.optimization_barrier((value, *earlier))[0]


def solution(mesh):
    forward, backward, across, sibling = routes(mesh)

    def move(x, pairs):
        return lax.ppermute(x, AXES, pairs)

    def shards(photo, text, sharpness, bias):
        rows = photo.shape[0]
        scale, offset = sharpness[0], bias[0]
        text_f = move(text, forward)
        text_b = move(text, backward)
        far = move(photo, across)
        near = move(photo, sibling)
        far_near = move(far, sibling)
        p = jnp.concatenate([photo, far, far_near, near], axis=0)
        r = jnp.arange(4 * rows, dtype=jnp.int32)[:, None]
        c = jnp.arange(2 * rows, dtype=jnp.int32)[None, :]
        label = jnp.where((r == c) & (r < rows), jnp.float32(1), jnp.float32(-1))
        texts = jnp.concatenate([text, text_f], axis=0)
        logit = scale * dot(p, texts, ((1,), (1,))) + offset
        g = -label * jax.nn.sigmoid(-label * logit) * scale
        text_b, g = lax.optimization_barrier((text_b, g))
        logit = scale * dot(p, text_b, ((1,), (1,))) + offset
        g = jnp.concatenate([g, jax.nn.sigmoid(logit) * scale], axis=1)
        texts = jnp.concatenate([texts, text_b], axis=0)
        p_far = dot(g[rows : 3 * rows], texts, ((1,), (0,)))
        far_near_back = move(p_far[rows:], sibling)
        t_fb = dot(g[:, rows:], p, ((0,), (0,)))
        b_back = move(t_fb[rows:], forward)
        p_across = p_far[:rows] + after(far_near_back, t_fb)
        far_back = move(p_across, across)
        f_back = move(after(t_fb[:rows], p_across), backward)
        g = after(g, p_across)
        p_near = dot(g[3 * rows :], texts, ((1,), (0,)))
        near_back = move(p_near, sibling)
        g = after(g, p_near)
        p_own = dot(g[:rows], texts, ((1,), (0,)))
        t_own = dot(after(g, p_own)[:, :rows], p, ((0,), (0,)))
        t_own, b_back, far_back, f_back = lax.optimization_barrier((t_own, b_back, far_back, f_back))
        return p_own + near_back + far_back, t_own + b_back + f_back

    spec = P(AXES, None)
    return jax.shard_map(shards, mesh=mesh, in_specs=(spec, spec, P(), P()), out_specs=(spec, spec), check_vma=False)
```
